32 devices in a mesh: dp: 4 (over z), sx: 4 (over x, core), sy: 2 (over y).
Axes of the slice: x: 2, y: 2, z: 4, core: 2. Of those that a mesh axis runs over, the one named last changes fastest.
Arguments:
- features: bfloat16 [4, 4, 2, 3072, 128], P('dp', 'sx', 'sy'), may hold values from -6 to 6
- cotangent: bfloat16 [4, 4, 2, 3072, 128], P('dp', 'sx', 'sy'), may hold values from -6 to 6
- weights: bfloat16 [27, 128, 128], replicated, may hold values from -0.109375 to 0.109375
- tables: int32 [4, 4, 2, 27, 24], P('dp', 'sx', 'sy'), may hold values from 0 to 56, as said below
- send_lists: int32 [4, 4, 2, 4], P('dp', 'sx', 'sy'), may hold values from 0 to 23, as said below
- counts: int32 [4, 4, 2], P('dp', 'sx', 'sy'), may hold values from 6 to 24, as said below
Outputs:
- output: bfloat16 [4, 4, 2, 3072, 128], P('dp', 'sx', 'sy')
- input_grad: bfloat16 [4, 4, 2, 3072, 128], P('dp', 'sx', 'sy')
- weight_grad: float32 [27, 128, 128], replicated
The draws below stay inside these ranges and needn't reach their ends.
Inputs may be any that keep to these rules, and one draw needn't show every extreme that they name: `tables`: entries below 24 name a block of the tile, 24 + n * 4 + s' the s'-th sent block of neighbour direction n, 56 the empty block; under offset 27 // 2 every block reads itself. `send_lists`: the 4 blocks of one tile are distinct. `counts`: some tile has all 24 blocks active.
All inputs are finite; a program needn't handle non-finite values.
Results may differ from the reference program's by a relative error of at most 0.001.
Values may be sent and summed in bfloat16 or wider, within the bound.
No kernel may reach another device: no remote copies, remote signals or barrier semaphores. Data moves between devices by JAX's collectives and lax.ppermute only.
A program may use at most 64 MiB of HBM per device.

```python
import math
import jax
import jax.numpy as jnp
from jax import lax

C = 128
K = 27
BV = 128
NB = 24
NS = 4
SCENES = 4
TX = 4
TY = 2
VOX = 3072
NE = 57
TOTAL_VOX = 98304


def draw_tables(key, part):
    key_kind, key_local, key_halo = jax.random.split(key, 3)
    shape = (SCENES, TX, TY, K, NB)
    kinds = jax.random.randint(key_kind, shape, 0, 10)
    local_pick = jax.random.randint(key_local, shape, 0, NB)
    halo_pick = NB + jax.random.randint(key_halo, shape, 0, 8 * NS)
    empty_pick = jnp.full(shape, NB + 8 * NS, jnp.int32)
    picks = jnp.where(kinds < 5, local_pick, jnp.where(kinds < 8, halo_pick, empty_pick))
    centre = jnp.broadcast_to(jnp.arange(NB, dtype=jnp.int32), shape)
    offset_ids = jnp.broadcast_to(jnp.arange(K, dtype=jnp.int32)[:, None], shape)
    picks = jnp.where(offset_ids == K // 2, centre, picks)
    return picks.astype(jnp.int32)


def draw_send_lists(key, part):
    scores = jax.random.randint(key, (SCENES, TX, TY, NB), 0, 4096) * NB + jnp.arange(NB, dtype=jnp.int32)
    order = jnp.argsort(scores, axis=-1, stable=True)
    return order[..., :NS].astype(jnp.int32)


def draw_counts(key, part):
    key_count, key_full = jax.random.split(key, 2)
    shape = (SCENES, TX, TY)
    values = jax.random.randint(key_count, shape, max(NB // 4, 1), NB + 1)
    full_tile = jax.random.randint(key_full, (), 0, SCENES * TX * TY)
    tile_ids = jnp.arange(SCENES * TX * TY, dtype=jnp.int32).reshape(shape)
    return jnp.where(tile_ids == full_tile, NB, values).astype(jnp.int32)


def shard_levels(own_key, shape, cuts, smallest, largest):
    def one(dim, shards_of):
        steps = jax.random.uniform(jax.random.fold_in(jax.random.fold_in(own_key, 6), dim), (shards_of,), jnp.float32, smallest / len(cuts), largest / len(cuts))
        return jnp.repeat(jnp.exp(steps), shape[dim] // shards_of).reshape((-1,) + (1,) * (len(shape) - dim - 1))

    loudness = one(*cuts[0])
    for cut in cuts[1:]:
        loudness = loudness * one(*cut)
    return loudness


def scatter_about(key, shape, deviation, bound, cuts=(), kind=jnp.bfloat16):
    factor_of = shard_levels(key, shape, cuts, -0.22, 0.18) if cuts else 1.0
    array = jax.random.normal(key, shape, jnp.float32) * deviation * factor_of
    return jnp.minimum(jnp.maximum(array, -bound), bound).astype(kind)


def setup_inputs(seed: int = 0) -> dict:
    splits = jax.random.split(jax.random.key(seed), 7)
    return {
        "features": scatter_about(splits[0], (SCENES, TX, TY, VOX, C), 1.0, 6.0, ((0, 4), (1, 4), (2, 2))),
        "cotangent": scatter_about(splits[1], (SCENES, TX, TY, VOX, C), 1.0, 6.0, ((0, 4), (1, 4), (2, 2))),
        "weights": scatter_about(splits[2], (K, C, C), (K * C) ** -0.5, 0.109375),
        "tables": draw_tables(jax.random.fold_in(splits[6], 71), 0),
        "send_lists": draw_send_lists(jax.random.fold_in(splits[6], 71), 0),
        "counts": draw_counts(jax.random.fold_in(splits[6], 71), 0),
    }


directions = ((-1, -1), (-1, 0), (-1, 1), (0, -1), (0, 1), (1, -1), (1, 0), (1, 1))

def device_pass(weight_sum, item):
    extended, blocks_grad, offset_table, weights = item
    weight_full = weights.astype(jnp.float32)
    gathered = extended[offset_table].astype(jnp.float32)
    grad_full = blocks_grad.astype(jnp.float32)
    hp = lax.Precision.HIGHEST
    outputs = jnp.einsum('kovc,kcd->ovd', gathered, weight_full, precision=hp)
    weight_part = jnp.einsum('kovc,ovd->kcd', gathered, grad_full, precision=hp)
    contrib = jnp.einsum('ovd,kcd->kovc', grad_full, weight_full, precision=hp)
    grad_ext = jnp.zeros((NE, BV, C), jnp.float32).at[offset_table.reshape(-1)].add(contrib.reshape(K * NB, BV, C))
    return (weight_sum + weight_part, (outputs, grad_ext))

def add_back(local_grad, sent_ids, portion):
    return local_grad.at[sent_ids].add(portion)

def reference(features, cotangent, weights, tables, send_lists, counts):
    devices = SCENES * TX * TY
    active = (jnp.arange(NB)[None, None, None, :] < counts[..., None]).astype(jnp.bfloat16)[..., None, None]
    blocks_in = features.reshape(SCENES, TX, TY, NB, BV, C) * active
    blocks_grad = cotangent.reshape(SCENES, TX, TY, NB, BV, C) * active
    sent = jnp.take_along_axis(blocks_in, send_lists[..., None, None], axis=3)
    padded = jnp.pad(sent, ((0, 0), (1, 1), (1, 1), (0, 0), (0, 0), (0, 0)))
    neighbours = [padded[:, 1 + step_x:1 + step_x + TX, 1 + step_y:1 + step_y + TY] for step_x, step_y in directions]
    extended = jnp.concatenate([blocks_in] + neighbours + [jnp.zeros((SCENES, TX, TY, 1, BV, C), jnp.bfloat16)], axis=3)
    weight_stack = jnp.broadcast_to(weights[None], (devices, K, C, C))
    weight_sum, (outputs, grad_ext) = lax.scan(device_pass, jnp.zeros((K, C, C), jnp.float32), (extended.reshape(devices, NE, BV, C), blocks_grad.reshape(devices, NB, BV, C), tables.reshape(devices, K, NB), weight_stack))
    active_full = active.astype(jnp.float32)
    output = (outputs.reshape(SCENES, TX, TY, NB, BV, C) * active_full).astype(jnp.bfloat16).reshape(features.shape)
    grad_ext = grad_ext.reshape(SCENES, TX, TY, NE, BV, C)
    halo_grads = grad_ext[:, :, :, NB:NB + 8 * NS].reshape(SCENES, TX, TY, 8, NS, BV, C)
    halo_padded = jnp.pad(halo_grads, ((0, 0), (1, 1), (1, 1), (0, 0), (0, 0), (0, 0), (0, 0)))
    returned = jnp.zeros((SCENES, TX, TY, NS, BV, C), jnp.float32)
    for slot_index, (step_x, step_y) in enumerate(directions):
        returned = returned + halo_padded[:, 1 - step_x:1 - step_x + TX, 1 - step_y:1 - step_y + TY, slot_index]
    local_grad = jax.vmap(add_back)(grad_ext[:, :, :, :NB].reshape(devices, NB, BV, C), send_lists.reshape(devices, NS), returned.reshape(devices, NS, BV, C))
    input_grad = (local_grad.reshape(SCENES, TX, TY, NB, BV, C) * active_full).astype(jnp.bfloat16).reshape(features.shape)
    weight_grad = weight_sum * (1.0 / math.sqrt(TOTAL_VOX))
    return (output, input_grad, weight_grad)
```

```python
import functools
import math

import jax
import jax.numpy as jnp
from jax import lax
from jax.experimental import pallas as pl
from jax.experimental.pallas import tpu as pltpu
from jax.sharding import PartitionSpec as P

AXES = ("dp", "sx", "sy")
F32 = jnp.float32
BF16 = jnp.bfloat16
VMEM = pl.BlockSpec(memory_space=pltpu.VMEM)
SMEM = pl.BlockSpec(memory_space=pltpu.SMEM)
HBM = pl.BlockSpec(memory_space=pl.ANY)


def params():
    return pltpu.CompilerParams(vmem_limit_bytes=24 * 2**20)


def cost(flops):
    return pl.CostEstimate(flops=flops, bytes_accessed=4 * 2**20, transcendentals=0)


def outgoing_kernel(sent_ref, count_ref, x_ref, out_ref, sems):
    num_sent = out_ref.shape[0]
    copies = [
        pltpu.make_async_copy(x_ref.at[sent_ref[s]], out_ref.at[s], sems.at[s])
        for s in range(num_sent)
    ]
    for copy in copies:
        copy.start()
    for copy in copies:
        copy.wait()
    for s in range(num_sent):

        @pl.when(sent_ref[s] >= count_ref[0])
        def _():
            out_ref[s] = jnp.zeros(out_ref.shape[1:], out_ref.dtype)


def outgoing(sent_ids, count, blocks):
    num_sent = sent_ids.shape[0]
    return pl.pallas_call(
        outgoing_kernel,
        out_shape=jax.ShapeDtypeStruct((num_sent,) + blocks.shape[1:], blocks.dtype),
        in_specs=[SMEM, SMEM, HBM],
        out_specs=VMEM,
        scratch_shapes=[pltpu.SemaphoreType.DMA((num_sent,))],
        compiler_params=params(),
    )(sent_ids, count, blocks)


def input_terms_kernel(picks, grad_ref, weight_ref, own_ref, *rest):
    *halo_refs, accum = rest
    num_blocks, rows, channels = grad_ref.shape
    offsets = weight_ref.shape[0] // channels
    accum[...] = jnp.zeros_like(accum)

    def term(o, matrix):
        return lax.dot_general(
            grad_ref[o], matrix, (((1,), (1,)), ((), ())), preferred_element_type=F32
        )

    def two_offsets(pair, carry):
        start = pl.multiple_of(pair * 2 * channels, 2 * channels)
        matrix = weight_ref[pl.ds(start, 2 * channels), :]
        for o in range(num_blocks):
            both = term(o, matrix)
            accum[picks[2 * pair * num_blocks + o]] += both[:, :channels]
            accum[picks[(2 * pair + 1) * num_blocks + o]] += both[:, channels:]
        return carry

    lax.fori_loop(0, offsets // 2, two_offsets, 0)
    if offsets % 2:
        matrix = weight_ref[(offsets - 1) * channels :, :]
        for o in range(num_blocks):
            accum[picks[(offsets - 1) * num_blocks + o]] += term(o, matrix)
    own_ref[...] = accum[:num_blocks]
    start = num_blocks
    for ref in halo_refs:
        ref[...] = accum[start : start + ref.shape[0]]
        start += ref.shape[0]


def input_terms(picks, grad, weights, halo_sizes):
    num_blocks, rows, channels = grad.shape
    sizes = (num_blocks,) + tuple(halo_sizes)
    return pl.pallas_call(
        input_terms_kernel,
        out_shape=[jax.ShapeDtypeStruct((n, rows, channels), F32) for n in sizes],
        in_specs=[SMEM, VMEM, VMEM],
        out_specs=[VMEM] * len(sizes),
        scratch_shapes=[pltpu.VMEM((sum(sizes) + 1, rows, channels), F32)],
        compiler_params=params(),
        cost_estimate=cost(10 * 10**9),
    )(picks, grad, weights.reshape(-1, channels))


def weight_terms_kernel(scale, chunks, me_ref, picks, grad_ref, *rest):
    *block_refs, keep_ref, send_ref, turned, accum = rest
    channels = grad_ref.shape[1]
    rows = block_refs[0].shape[1]
    num_blocks = grad_ref.shape[0] // rows
    offsets = accum.shape[0] // channels
    start = 0
    for ref in block_refs:
        for e in range(ref.shape[0]):
            turned[start + e] = ref[e].T
        start += ref.shape[0]
    turned[start] = jnp.zeros(turned.shape[1:], turned.dtype)
    accum[...] = jnp.zeros_like(accum)

    def two_blocks(pair, carry):
        first = pl.multiple_of(pair * 2 * rows, 2 * rows)
        grads = grad_ref[pl.ds(first, 2 * rows), :]
        for k in range(offsets):
            left = turned[picks[k * num_blocks + 2 * pair]]
            right = turned[picks[k * num_blocks + 2 * pair + 1]]
            accum[k * channels : (k + 1) * channels, :] += jnp.dot(
                jnp.concatenate([left, right], axis=1), grads, preferred_element_type=F32
            )
        return carry

    lax.fori_loop(0, num_blocks // 2, two_blocks, 0)
    size = accum.shape[0] // chunks
    for r in range(chunks):
        ref, place = (keep_ref, r) if r < chunks // 2 else (send_ref, r - chunks // 2)
        first = pl.multiple_of((me_ref[0] ^ r) * size, size)
        ref[place] = accum[pl.ds(first, size), :] * scale


def weight_terms(me, picks, grad, blocks, offsets, scale, chunks):
    num_blocks, rows, channels = grad.shape
    total = sum(b.shape[0] for b in blocks) + 1
    half = jax.ShapeDtypeStruct((chunks // 2, offsets * channels // chunks, channels), F32)
    return pl.pallas_call(
        functools.partial(weight_terms_kernel, scale, chunks),
        out_shape=[half, half],
        in_specs=[SMEM, SMEM, VMEM] + [VMEM] * len(blocks),
        out_specs=[VMEM, VMEM],
        scratch_shapes=[
            pltpu.VMEM((total, channels, rows), BF16),
            pltpu.VMEM((offsets * channels, channels), F32),
        ],
        compiler_params=params(),
        cost_estimate=cost(10 * 10**9),
    )(me, picks, grad.reshape(-1, channels), *blocks)


def output_kernel(group, picks, weight_ref, *rest):
    *block_refs, out_ref, held = rest
    total, rows, channels = held.shape
    offsets = weight_ref.shape[0] // channels
    num_blocks = out_ref.shape[0] // rows
    start = 0
    for ref in block_refs:
        held[start : start + ref.shape[0]] = ref[...]
        start += ref.shape[0]
    held[start] = jnp.zeros(held.shape[1:], held.dtype)

    def some_blocks(index, carry):
        accum = jnp.zeros((group * rows, channels), F32)
        for k in range(0, offsets, 2):
            pair = range(k, min(k + 2, offsets))
            gathered = [
                jnp.concatenate(
                    [held[picks[kk * num_blocks + index * group + j]] for kk in pair], axis=1
                )
                for j in range(group)
            ]
            accum += jnp.dot(
                jnp.concatenate(gathered, axis=0),
                weight_ref[k * channels : (k + len(pair)) * channels, :],
                preferred_element_type=F32,
            )
        first = pl.multiple_of(index * group * rows, group * rows)
        out_ref[pl.ds(first, group * rows), :] = accum.astype(BF16)
        return carry

    lax.fori_loop(0, num_blocks // group, some_blocks, 0)


def output_blocks(picks, weights, blocks):
    num_blocks, rows, channels = blocks[0].shape
    total = sum(b.shape[0] for b in blocks) + 1
    return pl.pallas_call(
        functools.partial(output_kernel, 4),
        out_shape=jax.ShapeDtypeStruct((num_blocks * rows, channels), BF16),
        in_specs=[SMEM, VMEM] + [VMEM] * len(blocks),
        out_specs=VMEM,
        scratch_shapes=[pltpu.VMEM((total, rows, channels), BF16)],
        compiler_params=params(),
        cost_estimate=cost(10 * 10**9),
    )(picks, weights.reshape(-1, channels), *blocks)


def input_grad_kernel(sent_ref, count_ref, own_ref, *rest):
    *returned_refs, out_ref = rest
    num_blocks = own_ref.shape[0]
    for b in range(num_blocks):
        keep = jnp.where(b < count_ref[0], 1.0, 0.0)
        out_ref[b] = (own_ref[b] * keep).astype(BF16)
    for s in range(returned_refs[0].shape[0]):
        b = sent_ref[s]
        keep = jnp.where(b < count_ref[0], 1.0, 0.0)
        returned = returned_refs[0][s]
        for ref in returned_refs[1:]:
            returned = returned + ref[s]
        out_ref[b] = ((own_ref[b] + returned) * keep).astype(BF16)


def input_grad_blocks(sent_ids, count, own, returned):
    return pl.pallas_call(
        input_grad_kernel,
        out_shape=jax.ShapeDtypeStruct(own.shape, BF16),
        in_specs=[SMEM, SMEM, VMEM] + [VMEM] * len(returned),
        out_specs=VMEM,
        compiler_params=params(),
        cost_estimate=cost(10**9),
    )(sent_ids, count, own, *returned)


def assemble_kernel(me_ref, near_ref, far_ref, out_ref, sems):
    half = near_ref.shape[0]
    copies = []
    for r in range(2 * half):
        source = near_ref.at[r] if r < half else far_ref.at[r - half]
        copies.append(pltpu.make_async_copy(source, out_ref.at[me_ref[0] ^ r], sems.at[r]))
    for copy in copies:
        copy.start()
    for copy in copies:
        copy.wait()


def assemble(me, near, far):
    half, size, channels = near.shape
    return pl.pallas_call(
        assemble_kernel,
        out_shape=jax.ShapeDtypeStruct((2 * half, size, channels), F32),
        in_specs=[SMEM, HBM, HBM],
        out_specs=HBM,
        scratch_shapes=[pltpu.SemaphoreType.DMA((2 * half,))],
        compiler_params=params(),
    )(me, near, far)


def local(features, cotangent, weights, tables, send_lists, counts):
    num_blocks = tables.shape[4]
    num_sent = send_lists.shape[3]
    offsets, channels = weights.shape[0], weights.shape[1]
    width = features.shape[3] // num_blocks
    size_z, size_x, size_y = (lax.axis_size(a) for a in AXES)
    scene, tile_x, tile_y = (lax.axis_index(a) for a in AXES)
    blocks = features.reshape(num_blocks, width, channels)
    grads = cotangent.reshape(num_blocks, width, channels)
    sent_ids = send_lists.reshape(num_sent)
    count = counts.reshape(1)

    odd = tile_x % 2
    inner = [(i, i ^ 1) for i in range(size_x) if (i ^ 1) < size_x]
    outer = [(i, i + 1) for i in range(1, size_x - 1, 2)]
    outer = outer + [(j, i) for i, j in outer]
    if size_y == 2:
        along_y = [[(0, 1), (1, 0)]]
    else:
        along_y = [
            [(i, i + 1) for i in range(size_y - 1)],
            [(i + 1, i) for i in range(size_y - 1)],
        ]
    sides = len(along_y)
    per_x = (1 + sides) * num_sent

    def to_blocks(array):
        return array.reshape(-1, width, channels)

    def to_rows(array):
        return array.reshape(-1, channels)

    table = tables.reshape(offsets, num_blocks)
    code = table - num_blocks
    number = code // num_sent
    cell = number + (number >= 4)
    step_x, step_y = cell // 3 - 1, cell % 3 - 1
    slot = code % num_sent
    near_x, near_y = tile_x + step_x, tile_y + step_y
    inside = (near_x >= 0) & (near_x < size_x) & (near_y >= 0) & (near_y < size_y)
    if size_y == 2:
        side = (step_y != 0).astype(jnp.int32)
    else:
        side = jnp.where(step_y == 0, 0, jnp.where(step_y < 0, 1, 2))
    toward = 1 - 2 * odd
    beyond_x = jnp.where(step_x == toward, 0, per_x) + sides * num_sent + side * num_sent + slot
    place = num_blocks + jnp.where(step_x == 0, (side - 1) * num_sent + slot, beyond_x)
    empty = num_blocks + sides * num_sent + 2 * per_x
    is_own = table < num_blocks
    is_empty = table >= num_blocks + 8 * num_sent
    place = jnp.where(is_own, table, place)
    dead = jnp.where(is_own, table >= count[0], is_empty | ~inside)
    dead = dead | (jnp.arange(num_blocks)[None] >= count[0])
    picks = jnp.where(dead, empty, place).astype(jnp.int32).reshape(-1)

    sent = to_rows(outgoing(sent_ids, count, blocks))
    beside = [lax.ppermute(sent, "sy", route) for route in along_y]
    column = jnp.concatenate([sent] + beside, axis=0)
    own_terms, *halo_terms = input_terms(
        picks, grads, weights, [num_sent] * sides + [per_x, per_x]
    )
    from_inner = lax.ppermute(column, "sx", inner)
    from_outer = lax.ppermute(column, "sx", outer)
    extended = [blocks] + [to_blocks(a) for a in beside + [from_inner, from_outer]]

    inner_back = lax.ppermute(to_rows(halo_terms[-2]), "sx", inner)
    outer_back = lax.ppermute(to_rows(halo_terms[-1]), "sx", outer)
    rows = num_sent * width
    returned = [inner_back[:rows], outer_back[:rows]]
    for number, route in enumerate(along_y):
        first, last = (1 + number) * rows, (2 + number) * rows
        portion = to_rows(halo_terms[number]) + inner_back[first:last] + outer_back[first:last]
        back = [(j, i) for i, j in route]
        returned.append(lax.ppermute(portion, "sy", back))

    scale = 1.0 / math.sqrt(num_blocks * width * size_z * size_x * size_y)
    if (size_z, size_x, size_y) == (4, 4, 2):
        me = (odd * 4 + (tile_x // 2) * 2 + tile_y).reshape(1)
        near, far = weight_terms(me, picks, grads, extended, offsets, scale, 8)

        def flat(z, x, y):
            return (z * size_x + x) * size_y + y

        def swap(array, dz, dx, dy):
            route = [
                (flat(z, x, y), flat(z ^ dz, x ^ dx, y ^ dy))
                for z in range(size_z)
                for x in range(size_x)
                for y in range(size_y)
            ]
            return lax.ppermute(array, AXES, route)

        near = near + swap(far, 0, 1, 0)
        shifts = ((0, 0, 1), (0, 2, 0), (0, 2, 1))
        part = near[0]
        for r, shift in enumerate(shifts):
            part = part + swap(near[r + 1], *shift)
        part = part + swap(part, 1, 0, 0)
        part = part + swap(part, 2, 0, 0)
        near = jnp.stack([part] + [swap(part, *shift) for shift in shifts])
        weight_grad = assemble(me, near, swap(near, 0, 1, 0)).reshape(weights.shape)
    else:
        zero = jnp.zeros((1,), jnp.int32)
        near, far = weight_terms(zero, picks, grads, extended, offsets, scale, 2)
        weight_grad = lax.psum(jnp.concatenate([near, far]).reshape(weights.shape), AXES)

    output = output_blocks(picks, weights, extended).reshape(features.shape)
    input_grad = input_grad_blocks(
        sent_ids, count, own_terms, [to_blocks(a) for a in returned]
    ).reshape(features.shape)
    return (output, input_grad, weight_grad)


def solution(mesh):
    tiles = P("dp", "sx", "sy", None, None)
    return jax.shard_map(
        local,
        mesh=mesh,
        in_specs=(tiles, tiles, P(), tiles, P("dp", "sx", "sy", None), P("dp", "sx", "sy")),
        out_specs=(tiles, tiles, P()),
        check_vma=False,
    )
```

```python
import functools
import math

import jax
import jax.numpy as jnp
from jax import lax
from jax.experimental import pallas as pl
from jax.experimental.pallas import tpu as pltpu
from jax.sharding import PartitionSpec as P

AXES = ("dp", "sx", "sy")
F32 = jnp.float32
BF16 = jnp.bfloat16
VMEM = pl.BlockSpec(memory_space=pltpu.VMEM)
SMEM = pl.BlockSpec(memory_space=pltpu.SMEM)
ANY = pl.BlockSpec(memory_space=pl.ANY)
HBM = pl.BlockSpec(memory_space=pltpu.HBM)


def params():
    return pltpu.CompilerParams(vmem_limit_bytes=12 * 2**20)


def cost(flops):
    return pl.CostEstimate(flops=flops, bytes_accessed=2**16, transcendentals=0)


def outgoing_kernel(sent_ref, count_ref, x_ref, out_ref, sems):
    num_sent = out_ref.shape[0]
    copies = [
        pltpu.make_async_copy(x_ref.at[sent_ref[s]], out_ref.at[s], sems.at[s])
        for s in range(num_sent)
    ]
    for copy in copies:
        copy.start()
    for copy in copies:
        copy.wait()
    for s in range(num_sent):

        @pl.when(sent_ref[s] >= count_ref[0])
        def _():
            out_ref[s] = jnp.zeros(out_ref.shape[1:], out_ref.dtype)


def outgoing(sent_ids, count, blocks):
    num_sent = sent_ids.shape[0]
    return pl.pallas_call(
        outgoing_kernel,
        out_shape=jax.ShapeDtypeStruct((num_sent,) + blocks.shape[1:], blocks.dtype),
        in_specs=[SMEM, SMEM, HBM],
        out_specs=VMEM,
        scratch_shapes=[pltpu.SemaphoreType.DMA((num_sent,))],
        compiler_params=params(),
        cost_estimate=pl.CostEstimate(flops=0, bytes_accessed=2**18, transcendentals=0),
    )(sent_ids, count, pltpu.with_memory_space_constraint(blocks, pltpu.HBM))


def input_terms_kernel(halo_spans, picks, grad_ref, weight_ref, own_ref, *rest):
    *halo_refs, accum = rest
    num_blocks, rows, channels = grad_ref.shape
    offsets = weight_ref.shape[0] // channels
    accum[...] = jnp.zeros_like(accum)

    def term(o, matrix):
        return lax.dot_general(
            grad_ref[o], matrix, (((1,), (1,)), ((), ())), preferred_element_type=F32
        )

    def two_offsets(pair, carry):
        start = pl.multiple_of(pair * 2 * channels, 2 * channels)
        matrix = weight_ref[pl.ds(start, 2 * channels), :]
        for o in range(num_blocks):
            both = term(o, matrix)
            accum[picks[o, 2 * pair]] += both[:, :channels]
            accum[picks[o, 2 * pair + 1]] += both[:, channels:]
        return carry

    lax.fori_loop(0, offsets // 2, two_offsets, 0)
    if offsets % 2:
        matrix = weight_ref[(offsets - 1) * channels :, :]
        for o in range(num_blocks):
            accum[picks[o, offsets - 1]] += term(o, matrix)
    own_ref[...] = accum[:num_blocks]
    for ref, spans in zip(halo_refs, halo_spans):
        to = 0
        for start, size in spans:
            ref[to : to + size] = accum[num_blocks + start : num_blocks + start + size]
            to += size


def input_terms(picks, grad, weights, halo_spans):
    num_blocks, rows, channels = grad.shape
    sizes = [num_blocks] + [sum(size for _, size in spans) for spans in halo_spans]
    return pl.pallas_call(
        functools.partial(input_terms_kernel, halo_spans),
        out_shape=[jax.ShapeDtypeStruct((n, rows, channels), F32) for n in sizes],
        in_specs=[SMEM, VMEM, VMEM],
        out_specs=[VMEM] * len(sizes),
        scratch_shapes=[pltpu.VMEM((sum(sizes) + 1, rows, channels), F32)],
        compiler_params=params(),
        cost_estimate=cost(10**7),
    )(picks, grad, weights.reshape(-1, channels))


def turn_kernel(block_ref, grad_ref, turned_ref, copy_ref):
    for e in range(block_ref.shape[0]):
        turned_ref[e] = block_ref[e].T
    copy_ref[...] = grad_ref[...]


def turn(blocks, grad):
    num_blocks, rows, channels = blocks.shape
    return pl.pallas_call(
        turn_kernel,
        out_shape=[
            jax.ShapeDtypeStruct((num_blocks, channels, rows), BF16),
            jax.ShapeDtypeStruct(grad.shape, BF16),
        ],
        in_specs=[VMEM, VMEM],
        out_specs=[VMEM, VMEM],
        compiler_params=params(),
        cost_estimate=cost(10**7),
    )(blocks, grad)


def weight_terms_kernel(scale, group, order_ref, picks, grad_ref, *rest):
    own_ref, *block_refs, out_ref, turned = rest
    channels = grad_ref.shape[1]
    rows = own_ref.shape[2]
    num_blocks = grad_ref.shape[0] // rows
    chunks, slots, size = out_ref.shape[:3]
    offsets = slots - 1
    start = own_ref.shape[0]
    turned[:start] = own_ref[...]
    for ref in block_refs:
        for e in range(ref.shape[0]):
            turned[start + e] = ref[e].T
        start += ref.shape[0]
    turned[start] = jnp.zeros(turned.shape[1:], turned.dtype)
    half = chunks * size
    lowest = order_ref[0]
    for r in range(1, chunks):
        lowest = jnp.minimum(lowest, order_ref[r])
    part = pl.ds(pl.multiple_of(lowest * size, half), half)

    def some_offsets(index, peak):
        wide = []
        for j in range(group):
            gathered = [turned[picks[o, index * group + j], part] for o in range(num_blocks)]
            wide.append(jnp.concatenate(gathered, axis=1))
        terms = jnp.dot(
            jnp.concatenate(wide, axis=0), grad_ref[...], preferred_element_type=F32
        )
        terms = (terms * scale).reshape(group, chunks, size, channels)
        for r in range(chunks):
            out_ref[order_ref[chunks + r], pl.ds(index * group, group)] = terms[:, r]
        return jnp.maximum(peak, jnp.max(jnp.abs(terms).reshape(-1, 8, channels), axis=0))

    peak = lax.fori_loop(
        0, offsets // group, some_offsets, jnp.zeros((8, channels), F32)
    )
    out_ref[:, offsets] = jnp.broadcast_to(jnp.max(peak), (chunks, size, channels))


def weight_terms(order, picks, grad, blocks, offsets, scale, chunks):
    num_blocks, rows, channels = grad.shape
    total = sum(b.shape[0] for b in blocks) + 1
    group = next(g for g in (9, 3, 1) if offsets % g == 0)
    size = channels // 8
    return pl.pallas_call(
        functools.partial(weight_terms_kernel, scale, group),
        out_shape=jax.ShapeDtypeStruct((chunks, offsets + 1, size, channels), F32),
        in_specs=[SMEM, SMEM, VMEM] + [VMEM] * len(blocks),
        out_specs=VMEM,
        scratch_shapes=[pltpu.VMEM((total, channels, rows), BF16)],
        compiler_params=params(),
        cost_estimate=cost(10**7),
    )(order, picks, grad.reshape(-1, channels), *blocks)


def output_kernel(group, span, done, picks, weight_ref, *rest):
    *block_refs, out_ref, held = rest
    if done:
        done_ref, *block_refs = block_refs
        out_ref[: done_ref.shape[0], :] = done_ref[...]
    total, rows, channels = held.shape
    offsets = weight_ref.shape[0] // channels
    start = 0
    for ref in block_refs:
        held[start : start + ref.shape[0]] = ref[...]
        start += ref.shape[0]
    held[start] = jnp.zeros(held.shape[1:], held.dtype)

    def some_blocks(index, carry):
        accum = jnp.zeros((group * rows, channels), F32)
        for k in range(0, offsets, 2):
            pair = range(k, min(k + 2, offsets))
            gathered = [
                jnp.concatenate(
                    [held[picks[index * group + j, kk]] for kk in pair], axis=1
                )
                for j in range(group)
            ]
            accum += jnp.dot(
                jnp.concatenate(gathered, axis=0),
                weight_ref[k * channels : (k + len(pair)) * channels, :],
                preferred_element_type=F32,
            )
        first = pl.multiple_of(index * group * rows, group * rows)
        out_ref[pl.ds(first, group * rows), :] = accum.astype(BF16)
        return carry

    lax.fori_loop(span[0] // group, span[1] // group, some_blocks, 0)


def output_blocks(picks, weights, blocks, span, done=()):
    _, rows, channels = blocks[0].shape
    total = sum(b.shape[0] for b in blocks) + 1
    group = next(g for g in (8, 6, 4, 2, 1) if span[0] % g == span[1] % g == 0)
    return pl.pallas_call(
        functools.partial(output_kernel, group, span, len(done)),
        out_shape=jax.ShapeDtypeStruct((span[1] * rows, channels), BF16),
        in_specs=[SMEM, VMEM] + [VMEM] * (len(done) + len(blocks)),
        out_specs=VMEM,
        scratch_shapes=[pltpu.VMEM((total, rows, channels), BF16)],
        compiler_params=params(),
        cost_estimate=cost(10**7),
    )(picks, weights.reshape(-1, channels), *done, *blocks)


def input_grad_kernel(sent_ref, count_ref, own_ref, *rest):
    *returned_refs, out_ref = rest
    num_blocks = own_ref.shape[0]
    for b in range(num_blocks):
        keep = jnp.where(b < count_ref[0], 1.0, 0.0)
        out_ref[b] = (own_ref[b] * keep).astype(BF16)
    for s in range(returned_refs[0].shape[0]):
        b = sent_ref[s]
        keep = jnp.where(b < count_ref[0], 1.0, 0.0)
        returned = returned_refs[0][s]
        for ref in returned_refs[1:]:
            returned = returned + ref[s]
        out_ref[b] = ((own_ref[b] + returned) * keep).astype(BF16)


def input_grad_blocks(sent_ids, count, own, returned):
    return pl.pallas_call(
        input_grad_kernel,
        out_shape=jax.ShapeDtypeStruct(own.shape, BF16),
        in_specs=[SMEM, SMEM, VMEM] + [VMEM] * len(returned),
        out_specs=VMEM,
        compiler_params=params(),
        cost_estimate=cost(10**7),
    )(sent_ids, count, own, *returned)


def assemble_kernel(order_ref, *rest):
    *piece_refs, out_ref, sems = rest
    chunks = [ref.at[r] for ref in piece_refs for r in range(ref.shape[0])]
    size = chunks[0].shape[1]
    copies = []
    for r, chunk in enumerate(chunks):
        first = pl.multiple_of(order_ref[r] * size, size)
        copies.append(
            pltpu.make_async_copy(
                chunk.at[: out_ref.shape[0]], out_ref.at[:, pl.ds(first, size)], sems.at[r]
            )
        )
    for copy in copies:
        copy.start()
    for copy in copies:
        copy.wait()


def assemble(order, pieces):
    count = sum(p.shape[0] for p in pieces)
    _, slots, size, channels = pieces[0].shape
    return pl.pallas_call(
        assemble_kernel,
        out_shape=jax.ShapeDtypeStruct((slots - 1, count * size, channels), F32),
        in_specs=[SMEM] + [ANY] * len(pieces),
        out_specs=ANY,
        scratch_shapes=[pltpu.SemaphoreType.DMA((count,))],
        compiler_params=params(),
    )(order, *pieces)


def local(features, cotangent, weights, tables, send_lists, counts):
    num_blocks = tables.shape[4]
    num_sent = send_lists.shape[3]
    offsets, channels = weights.shape[0], weights.shape[1]
    width = features.shape[3] // num_blocks
    size_z, size_x, size_y = (lax.axis_size(a) for a in AXES)
    scene, tile_x, tile_y = (lax.axis_index(a) for a in AXES)
    blocks = features.reshape(num_blocks, width, channels)
    grads = cotangent.reshape(num_blocks, width, channels)
    sent_ids = send_lists.reshape(num_sent)
    count = counts.reshape(1)

    odd = tile_x % 2
    inner = [(i, i ^ 1) for i in range(size_x) if (i ^ 1) < size_x]
    outer = [(i, i + 1) for i in range(1, size_x - 1, 2)]
    outer = outer + [(j, i) for i, j in outer]
    if size_y == 2:
        along_y = [[(0, 1), (1, 0)]]
    else:
        along_y = [
            [(i, i + 1) for i in range(size_y - 1)],
            [(i + 1, i) for i in range(size_y - 1)],
        ]
    sides = len(along_y)
    per_x = (1 + sides) * num_sent
    paired = (size_z, size_x, size_y) == (4, 4, 2)

    def to_blocks(array):
        return array.reshape(-1, width, channels)

    def to_rows(array):
        return array.reshape(-1, channels)

    table = tables.reshape(offsets, num_blocks).T
    code = table - num_blocks
    number = code // num_sent
    cell = number + (number >= 4)
    step_x, step_y = cell // 3 - 1, cell % 3 - 1
    slot = code % num_sent
    near_x, near_y = tile_x + step_x, tile_y + step_y
    inside = (near_x >= 0) & (near_x < size_x) & (near_y >= 0) & (near_y < size_y)
    if size_y == 2:
        side = (step_y != 0).astype(jnp.int32)
    else:
        side = jnp.where(step_y == 0, 0, jnp.where(step_y < 0, 1, 2))
    toward = 1 - 2 * odd
    if paired:
        middle = (tile_x == 1) | (tile_x == 2)
        to_inner = jnp.where(side == 0, 0, jnp.where(middle, 3, 2))
        place = jnp.where(
            step_x == 0, jnp.where(middle, 4, 1), jnp.where(step_x == toward, to_inner, 1 + side)
        )
        place = num_blocks + place * num_sent + slot
        empty = num_blocks + 5 * num_sent
    else:
        beyond_x = jnp.where(step_x == toward, 0, per_x) + (sides + side) * num_sent + slot
        place = num_blocks + jnp.where(step_x == 0, (side - 1) * num_sent + slot, beyond_x)
        empty = num_blocks + sides * num_sent + 2 * per_x
    is_own = table < num_blocks
    is_empty = table >= num_blocks + 8 * num_sent
    place = jnp.where(is_own, table, place)
    dead = jnp.where(is_own, table >= count[0], is_empty | ~inside)
    dead = dead | (jnp.arange(num_blocks)[:, None] >= count[0])
    picks = jnp.where(dead, empty, place).astype(jnp.int32)

    sent = to_rows(outgoing(sent_ids, count, blocks))
    turned_own, kept_grads = turn(blocks, grads)
    scale = 1.0 / math.sqrt(num_blocks * width * size_z * size_x * size_y)
    if paired:

        def flat(z, x, c, y):
            return (z * size_x + 2 * x + c) * size_y + y

        def exchange(array, to, senders=lambda z, x, c, y: True):
            places = [
                (z, x, c, y) for z in range(4) for x in range(2) for c in range(2) for y in range(2)
            ]
            route = [(flat(*p), flat(*to(*p))) for p in places if senders(*p)]
            return lax.ppermute(array, AXES, route)

        def cores(z, x, c, y):
            return z, x, 1 - c, y

        def is_middle(z, x, c, y):
            return x != c

        def straight(z, x, c, y):
            return (z, 1 - x, 1 - c, y) if is_middle(z, x, c, y) else (z, x, c, 1 - y)

        def across(z, x, c, y):
            return (z, 1 - x, 1 - c, 1 - y) if is_middle(z, x, c, y) else (z, x, c, 1 - y)

        def is_end(*p):
            return not is_middle(*p)

        beside = exchange(sent, cores)
        first = exchange(sent, straight)
        second = exchange(jnp.where(middle, sent, beside), across)
        first, second, turned_own = lax.optimization_barrier((first, second, turned_own))
        passed = [exchange(first, cores, is_end), exchange(second, cores, is_end)]
        extended = [blocks] + [to_blocks(a) for a in [beside, first, second] + passed]

        core, far_x = odd, tile_x // 2
        chunk = jnp.arange(4, dtype=jnp.int32)
        low = far_x * 2 + tile_y
        swapped = (chunk % 2) * 2 + chunk // 2
        mine = jnp.where(core == 0, chunk, swapped)
        theirs = jnp.where(core == 0, swapped, chunk)
        keep, send = core * 4 + (low ^ mine), (1 - core) * 4 + (low ^ theirs)

        def places(bits):
            moved = chunk ^ low
            return jnp.where(bits == 0, moved, (moved % 2) * 2 + moved // 2)

        near_order = jnp.concatenate([core * 4 + chunk, places(core)])
        far_order = jnp.concatenate([(1 - core) * 4 + chunk, places(1 - core)])
        order = jnp.concatenate([keep, send])
        blocks_turned = [turned_own] + extended[1:]
        far = weight_terms(far_order, picks, kept_grads, blocks_turned, offsets, scale, 4)
        kept_grads, far = lax.optimization_barrier((kept_grads, far))
        near = weight_terms(near_order, picks, kept_grads, blocks_turned, offsets, scale, 4)

        def x_or_y(z, x, c, y):
            return (z, 1 - x, c, y) if c == 0 else (z, x, c, 1 - y)

        def y_or_x(z, x, c, y):
            return (z, x, c, 1 - y) if c == 0 else (z, 1 - x, c, y)

        def z_far(z, x, c, y):
            return (z ^ 2, x, c, y)

        def z_near(z, x, c, y):
            return (z ^ 1, x, c, y)

        slot_id = lax.broadcasted_iota(jnp.int32, (1, offsets + 1, 1, 1), 1)

        def encode(part):
            bound = jnp.maximum(part[:, offsets:], 1e-30)
            exponent = jnp.ceil(jnp.log2(bound)) - 15.0
            values = part * jnp.exp2(-exponent)
            return jnp.where(slot_id < offsets, values, exponent).astype(jnp.float16)

        def decode(message):
            wide = message.astype(F32)
            unit = jnp.exp2(wide[:, offsets:])
            return jnp.where(slot_id < offsets, wide * unit, unit * 32768.0)

        near = near + exchange(far, cores)
        message, pair = encode(near[2:]), near[:2]
        message, pair, late_grads = lax.optimization_barrier((message, pair, kept_grads))
        spans = [(r * num_sent, num_sent) for r in range(5)]
        own_terms, inner_terms, first_terms, second_terms = input_terms(
            picks, late_grads, weights, [[spans[0], spans[3], spans[4]], [spans[1]], [spans[2]]]
        )
        back = exchange(inner_terms, cores)
        pair = pair + decode(exchange(message, x_or_y))
        message, part, own_terms, late_picks = lax.optimization_barrier(
            (encode(pair[1:]), pair[:1], own_terms, picks)
        )
        middle_block = num_blocks // 2
        upper = output_blocks(late_picks, weights, extended, (0, middle_block))
        message = encode(part + decode(exchange(message, y_or_x)))
        message, back, upper = lax.optimization_barrier((message, back, upper))
        first_back = exchange(first_terms + back[num_sent : 2 * num_sent], straight)
        second_back = exchange(second_terms + back[2 * num_sent :], across)
        part = decode(message) + decode(exchange(message, z_far))
        message, late_picks, first_back, second_back = lax.optimization_barrier(
            (encode(part), late_picks, first_back, second_back)
        )
        output = output_blocks(
            late_picks, weights, extended, (middle_block, num_blocks), (upper,)
        )
        passed_back = exchange(second_back, cores, is_end)
        part = decode(message) + decode(exchange(message, z_near))
        returned = [
            back[:num_sent] + jnp.where(middle, second_back, 0.0),
            first_back,
            passed_back,
        ]
        message, output, own_terms = lax.optimization_barrier((encode(part), output, own_terms))
        input_grad = input_grad_blocks(sent_ids, count, own_terms, returned)
        pair = jnp.concatenate([message, exchange(message, y_or_x)])
        pair, input_grad = lax.optimization_barrier((pair, input_grad))
        rest = exchange(pair, x_or_y)
        messages = [pair, rest, exchange(pair, cores), exchange(rest, cores)]
        weight_grad = assemble(order, [decode(m) for m in messages])

    else:
        beside = [lax.ppermute(sent, "sy", route) for route in along_y]
        column = jnp.concatenate([sent] + beside, axis=0)
        from_inner = lax.ppermute(column, "sx", inner)
        from_outer = lax.ppermute(column, "sx", outer)
        extended = [blocks] + [to_blocks(a) for a in beside + [from_inner, from_outer]]
        order = jnp.concatenate([jnp.arange(8, dtype=jnp.int32)] * 2)
        parts = weight_terms(
            order, picks, kept_grads, [turned_own] + extended[1:], offsets, scale, 8
        )
        parts = jnp.swapaxes(parts[:, :offsets], 0, 1)
        weight_grad = lax.psum(parts.reshape(weights.shape), AXES)

        spans = [(r * num_sent, num_sent) for r in range(sides)]
        spans += [(sides * num_sent + r * per_x, per_x) for r in range(2)]
        own_terms, *halo_terms = input_terms(picks, grads, weights, [[span] for span in spans])
        inner_back = lax.ppermute(halo_terms[-2], "sx", inner)
        outer_back = lax.ppermute(halo_terms[-1], "sx", outer)
        returned = [inner_back[:num_sent], outer_back[:num_sent]]
        for number, route in enumerate(along_y):
            part = slice((1 + number) * num_sent, (2 + number) * num_sent)
            portion = halo_terms[number] + inner_back[part] + outer_back[part]
            returned.append(lax.ppermute(portion, "sy", [(j, i) for i, j in route]))
        output = output_blocks(picks, weights, extended, (0, num_blocks))
        input_grad = input_grad_blocks(sent_ids, count, own_terms, returned)

    return (output.reshape(features.shape), input_grad.reshape(features.shape), weight_grad)


def solution(mesh):
    tiles = P("dp", "sx", "sy", None, None)
    return jax.shard_map(
        local,
        mesh=mesh,
        in_specs=(tiles, tiles, P(), tiles, P("dp", "sx", "sy", None), P("dp", "sx", "sy")),
        out_specs=(tiles, tiles, P()),
        check_vma=False,
    )
```

```python
import functools
import math

import jax
import jax.numpy as jnp
from jax import lax
from jax.experimental import pallas as pl
from jax.experimental.pallas import tpu as pltpu
from jax.sharding import PartitionSpec as P

AXES = ("dp", "sx", "sy")
F32 = jnp.float32
BF16 = jnp.bfloat16
VMEM = pl.BlockSpec(memory_space=pltpu.VMEM)
SMEM = pl.BlockSpec(memory_space=pltpu.SMEM)
ANY = pl.BlockSpec(memory_space=pl.ANY)
HBM = pl.BlockSpec(memory_space=pltpu.HBM)


def params():
    return pltpu.CompilerParams(vmem_limit_bytes=12 * 2**20)


def cost(flops):
    return pl.CostEstimate(flops=flops, bytes_accessed=4 * 2**20, transcendentals=0)


def outgoing_kernel(sent_ref, count_ref, x_ref, out_ref, sems):
    num_sent = out_ref.shape[0]
    copies = [
        pltpu.make_async_copy(x_ref.at[sent_ref[s]], out_ref.at[s], sems.at[s])
        for s in range(num_sent)
    ]
    for copy in copies:
        copy.start()
    for copy in copies:
        copy.wait()
    for s in range(num_sent):

        @pl.when(sent_ref[s] >= count_ref[0])
        def _():
            out_ref[s] = jnp.zeros(out_ref.shape[1:], out_ref.dtype)


def outgoing(sent_ids, count, blocks):
    num_sent = sent_ids.shape[0]
    return pl.pallas_call(
        outgoing_kernel,
        out_shape=jax.ShapeDtypeStruct((num_sent,) + blocks.shape[1:], blocks.dtype),
        in_specs=[SMEM, SMEM, HBM],
        out_specs=VMEM,
        scratch_shapes=[pltpu.SemaphoreType.DMA((num_sent,))],
        compiler_params=params(),
        cost_estimate=pl.CostEstimate(flops=0, bytes_accessed=2**18, transcendentals=0),
    )(sent_ids, count, pltpu.with_memory_space_constraint(blocks, pltpu.HBM))


def input_terms_kernel(halo_spans, picks, grad_ref, weight_ref, own_ref, *rest):
    *halo_refs, accum = rest
    num_blocks, rows, channels = grad_ref.shape
    offsets = weight_ref.shape[0] // channels
    accum[...] = jnp.zeros_like(accum)

    def term(o, matrix):
        return lax.dot_general(
            grad_ref[o], matrix, (((1,), (1,)), ((), ())), preferred_element_type=F32
        )

    def two_offsets(pair, carry):
        start = pl.multiple_of(pair * 2 * channels, 2 * channels)
        matrix = weight_ref[pl.ds(start, 2 * channels), :]
        for o in range(num_blocks):
            both = term(o, matrix)
            accum[picks[o, 2 * pair]] += both[:, :channels]
            accum[picks[o, 2 * pair + 1]] += both[:, channels:]
        return carry

    lax.fori_loop(0, offsets // 2, two_offsets, 0)
    if offsets % 2:
        matrix = weight_ref[(offsets - 1) * channels :, :]
        for o in range(num_blocks):
            accum[picks[o, offsets - 1]] += term(o, matrix)
    own_ref[...] = accum[:num_blocks]
    for ref, spans in zip(halo_refs, halo_spans):
        to = 0
        for start, size in spans:
            ref[to : to + size] = accum[num_blocks + start : num_blocks + start + size]
            to += size


def input_terms(picks, grad, weights, halo_spans):
    num_blocks, rows, channels = grad.shape
    sizes = [num_blocks] + [sum(size for _, size in spans) for spans in halo_spans]
    return pl.pallas_call(
        functools.partial(input_terms_kernel, halo_spans),
        out_shape=[jax.ShapeDtypeStruct((n, rows, channels), F32) for n in sizes],
        in_specs=[SMEM, VMEM, VMEM],
        out_specs=[VMEM] * len(sizes),
        scratch_shapes=[pltpu.VMEM((sum(sizes) + 1, rows, channels), F32)],
        compiler_params=params(),
        cost_estimate=cost(10**7),
    )(picks, grad, weights.reshape(-1, channels))


def turn_kernel(block_ref, grad_ref, turned_ref, copy_ref):
    for e in range(block_ref.shape[0]):
        turned_ref[e] = block_ref[e].T
    copy_ref[...] = grad_ref[...]


def turn(blocks, grad):
    num_blocks, rows, channels = blocks.shape
    return pl.pallas_call(
        turn_kernel,
        out_shape=[
            jax.ShapeDtypeStruct((num_blocks, channels, rows), BF16),
            jax.ShapeDtypeStruct(grad.shape, BF16),
        ],
        in_specs=[VMEM, VMEM],
        out_specs=[VMEM, VMEM],
        compiler_params=params(),
        cost_estimate=cost(10**7),
    )(blocks, grad)


def weight_terms_kernel(scale, group, order_ref, picks, grad_ref, *rest):
    own_ref, *block_refs, out_ref, turned = rest
    channels = grad_ref.shape[1]
    rows = own_ref.shape[2]
    num_blocks = grad_ref.shape[0] // rows
    chunks, slots, size = out_ref.shape[:3]
    offsets = slots - 1
    start = own_ref.shape[0]
    turned[:start] = own_ref[...]
    for ref in block_refs:
        for e in range(ref.shape[0]):
            turned[start + e] = ref[e].T
        start += ref.shape[0]
    turned[start] = jnp.zeros(turned.shape[1:], turned.dtype)
    half = chunks * size
    lowest = order_ref[0]
    for r in range(1, chunks):
        lowest = jnp.minimum(lowest, order_ref[r])
    part = pl.ds(pl.multiple_of(lowest * size, half), half)

    def some_offsets(index, peak):
        wide = []
        for j in range(group):
            gathered = [turned[picks[o, index * group + j], part] for o in range(num_blocks)]
            wide.append(jnp.concatenate(gathered, axis=1))
        terms = jnp.dot(
            jnp.concatenate(wide, axis=0), grad_ref[...], preferred_element_type=F32
        )
        terms = (terms * scale).reshape(group, chunks, size, channels)
        for r in range(chunks):
            out_ref[order_ref[chunks + r], pl.ds(index * group, group)] = terms[:, r]
        return jnp.maximum(peak, jnp.max(jnp.abs(terms).reshape(-1, 8, channels), axis=0))

    peak = lax.fori_loop(
        0, offsets // group, some_offsets, jnp.zeros((8, channels), F32)
    )
    out_ref[:, offsets] = jnp.broadcast_to(jnp.max(peak), (chunks, size, channels))


def weight_terms(order, picks, grad, blocks, offsets, scale, chunks):
    num_blocks, rows, channels = grad.shape
    total = sum(b.shape[0] for b in blocks) + 1
    group = next(g for g in (9, 3, 1) if offsets % g == 0)
    size = channels // 8
    return pl.pallas_call(
        functools.partial(weight_terms_kernel, scale, group),
        out_shape=jax.ShapeDtypeStruct((chunks, offsets + 1, size, channels), F32),
        in_specs=[SMEM, SMEM, VMEM] + [VMEM] * len(blocks),
        out_specs=VMEM,
        scratch_shapes=[pltpu.VMEM((total, channels, rows), BF16)],
        compiler_params=params(),
        cost_estimate=cost(10**7),
    )(order, picks, grad.reshape(-1, channels), *blocks)


def output_kernel(group, span, done, picks, weight_ref, *rest):
    *block_refs, out_ref, held = rest
    if done:
        done_ref, *block_refs = block_refs
        out_ref[: done_ref.shape[0], :] = done_ref[...]
    total, rows, channels = held.shape
    offsets = weight_ref.shape[0] // channels
    start = 0
    for ref in block_refs:
        held[start : start + ref.shape[0]] = ref[...]
        start += ref.shape[0]
    held[start] = jnp.zeros(held.shape[1:], held.dtype)

    def some_blocks(index, carry):
        accum = jnp.zeros((group * rows, channels), F32)
        for k in range(0, offsets, 2):
            pair = range(k, min(k + 2, offsets))
            gathered = [
                jnp.concatenate(
                    [held[picks[index * group + j, kk]] for kk in pair], axis=1
                )
                for j in range(group)
            ]
            accum += jnp.dot(
                jnp.concatenate(gathered, axis=0),
                weight_ref[k * channels : (k + len(pair)) * channels, :],
                preferred_element_type=F32,
            )
        first = pl.multiple_of(index * group * rows, group * rows)
        out_ref[pl.ds(first, group * rows), :] = accum.astype(BF16)
        return carry

    lax.fori_loop(span[0] // group, span[1] // group, some_blocks, 0)


def output_blocks(picks, weights, blocks, span, done=()):
    _, rows, channels = blocks[0].shape
    total = sum(b.shape[0] for b in blocks) + 1
    group = next(g for g in (8, 6, 4, 2, 1) if span[0] % g == span[1] % g == 0)
    return pl.pallas_call(
        functools.partial(output_kernel, group, span, len(done)),
        out_shape=jax.ShapeDtypeStruct((span[1] * rows, channels), BF16),
        in_specs=[SMEM, VMEM] + [VMEM] * (len(done) + len(blocks)),
        out_specs=VMEM,
        scratch_shapes=[pltpu.VMEM((total, rows, channels), BF16)],
        compiler_params=params(),
        cost_estimate=cost(10**7),
    )(picks, weights.reshape(-1, channels), *done, *blocks)


def input_grad_kernel(sent_ref, count_ref, own_ref, *rest):
    *returned_refs, out_ref = rest
    num_blocks = own_ref.shape[0]
    for b in range(num_blocks):
        keep = jnp.where(b < count_ref[0], 1.0, 0.0)
        out_ref[b] = (own_ref[b] * keep).astype(BF16)
    for s in range(returned_refs[0].shape[0]):
        b = sent_ref[s]
        keep = jnp.where(b < count_ref[0], 1.0, 0.0)
        returned = returned_refs[0][s]
        for ref in returned_refs[1:]:
            returned = returned + ref[s]
        out_ref[b] = ((own_ref[b] + returned) * keep).astype(BF16)


def input_grad_blocks(sent_ids, count, own, returned):
    return pl.pallas_call(
        input_grad_kernel,
        out_shape=jax.ShapeDtypeStruct(own.shape, BF16),
        in_specs=[SMEM, SMEM, VMEM] + [VMEM] * len(returned),
        out_specs=VMEM,
        compiler_params=params(),
        cost_estimate=cost(10**7),
    )(sent_ids, count, own, *returned)


def assemble_kernel(order_ref, *rest):
    *piece_refs, out_ref, sems = rest
    chunks = [ref.at[r] for ref in piece_refs for r in range(ref.shape[0])]
    size = chunks[0].shape[1]
    copies = []
    for r, chunk in enumerate(chunks):
        first = pl.multiple_of(order_ref[r] * size, size)
        copies.append(
            pltpu.make_async_copy(
                chunk.at[: out_ref.shape[0]], out_ref.at[:, pl.ds(first, size)], sems.at[r]
            )
        )
    for copy in copies:
        copy.start()
    for copy in copies:
        copy.wait()


def assemble(order, pieces):
    count = sum(p.shape[0] for p in pieces)
    _, slots, size, channels = pieces[0].shape
    return pl.pallas_call(
        assemble_kernel,
        out_shape=jax.ShapeDtypeStruct((slots - 1, count * size, channels), F32),
        in_specs=[SMEM] + [ANY] * len(pieces),
        out_specs=ANY,
        scratch_shapes=[pltpu.SemaphoreType.DMA((count,))],
        compiler_params=params(),
    )(order, *pieces)


def local(features, cotangent, weights, tables, send_lists, counts):
    num_blocks = tables.shape[4]
    num_sent = send_lists.shape[3]
    offsets, channels = weights.shape[0], weights.shape[1]
    width = features.shape[3] // num_blocks
    size_z, size_x, size_y = (lax.axis_size(a) for a in AXES)
    scene, tile_x, tile_y = (lax.axis_index(a) for a in AXES)
    blocks = features.reshape(num_blocks, width, channels)
    grads = cotangent.reshape(num_blocks, width, channels)
    sent_ids = send_lists.reshape(num_sent)
    count = counts.reshape(1)

    odd = tile_x % 2
    inner = [(i, i ^ 1) for i in range(size_x) if (i ^ 1) < size_x]
    outer = [(i, i + 1) for i in range(1, size_x - 1, 2)]
    outer = outer + [(j, i) for i, j in outer]
    if size_y == 2:
        along_y = [[(0, 1), (1, 0)]]
    else:
        along_y = [
            [(i, i + 1) for i in range(size_y - 1)],
            [(i + 1, i) for i in range(size_y - 1)],
        ]
    sides = len(along_y)
    per_x = (1 + sides) * num_sent
    paired = (size_z, size_x, size_y) == (4, 4, 2)

    def to_blocks(array):
        return array.reshape(-1, width, channels)

    def to_rows(array):
        return array.reshape(-1, channels)

    table = tables.reshape(offsets, num_blocks).T
    code = table - num_blocks
    number = code // num_sent
    cell = number + (number >= 4)
    step_x, step_y = cell // 3 - 1, cell % 3 - 1
    slot = code % num_sent
    near_x, near_y = tile_x + step_x, tile_y + step_y
    inside = (near_x >= 0) & (near_x < size_x) & (near_y >= 0) & (near_y < size_y)
    if size_y == 2:
        side = (step_y != 0).astype(jnp.int32)
    else:
        side = jnp.where(step_y == 0, 0, jnp.where(step_y < 0, 1, 2))
    toward = 1 - 2 * odd
    if paired:
        middle = (tile_x == 1) | (tile_x == 2)
        to_inner = jnp.where(side == 0, 0, jnp.where(middle, 3, 2))
        place = jnp.where(
            step_x == 0, jnp.where(middle, 4, 1), jnp.where(step_x == toward, to_inner, 1 + side)
        )
        place = num_blocks + place * num_sent + slot
        empty = num_blocks + 5 * num_sent
    else:
        beyond_x = jnp.where(step_x == toward, 0, per_x) + (sides + side) * num_sent + slot
        place = num_blocks + jnp.where(step_x == 0, (side - 1) * num_sent + slot, beyond_x)
        empty = num_blocks + sides * num_sent + 2 * per_x
    is_own = table < num_blocks
    is_empty = table >= num_blocks + 8 * num_sent
    place = jnp.where(is_own, table, place)
    dead = jnp.where(is_own, table >= count[0], is_empty | ~inside)
    dead = dead | (jnp.arange(num_blocks)[:, None] >= count[0])
    picks = jnp.where(dead, empty, place).astype(jnp.int32)

    sent = to_rows(outgoing(sent_ids, count, blocks))
    turned_own, kept_grads = turn(blocks, grads)
    scale = 1.0 / math.sqrt(num_blocks * width * size_z * size_x * size_y)
    if paired:

        def flat(z, x, c, y):
            return (z * size_x + 2 * x + c) * size_y + y

        def exchange(array, to):
            places = [
                (z, x, c, y) for z in range(4) for x in range(2) for c in range(2) for y in range(2)
            ]
            route = [(flat(*p), flat(*to(*p))) for p in places]
            return lax.ppermute(array, AXES, route)

        def cores(z, x, c, y):
            return z, x, 1 - c, y

        def is_middle(z, x, c, y):
            return x != c

        def straight(z, x, c, y):
            return (z, 1 - x, 1 - c, y) if is_middle(z, x, c, y) else (z, x, c, 1 - y)

        def across(z, x, c, y):
            return (z, 1 - x, 1 - c, 1 - y) if is_middle(z, x, c, y) else (z, x, c, 1 - y)

        beside = exchange(sent, cores)
        first = exchange(sent, straight)
        second = exchange(jnp.where(middle, sent, beside), across)
        first, second, turned_own = lax.optimization_barrier((first, second, turned_own))
        passed = [exchange(first, cores), exchange(second, cores)]
        extended = [blocks] + [to_blocks(a) for a in [beside, first, second] + passed]

        core, far_x = odd, tile_x // 2
        chunk = jnp.arange(4, dtype=jnp.int32)
        low = far_x * 2 + tile_y
        swapped = (chunk % 2) * 2 + chunk // 2
        mine = jnp.where(core == 0, chunk, swapped)
        theirs = jnp.where(core == 0, swapped, chunk)
        keep, send = core * 4 + (low ^ mine), (1 - core) * 4 + (low ^ theirs)

        def places(bits):
            moved = chunk ^ low
            return jnp.where(bits == 0, moved, (moved % 2) * 2 + moved // 2)

        near_order = jnp.concatenate([core * 4 + chunk, places(core)])
        far_order = jnp.concatenate([(1 - core) * 4 + chunk, places(1 - core)])
        order = jnp.concatenate([keep, send])
        blocks_turned = [turned_own] + extended[1:]
        far = weight_terms(far_order, picks, kept_grads, blocks_turned, offsets, scale, 4)
        kept_grads, far = lax.optimization_barrier((kept_grads, far))
        near = weight_terms(near_order, picks, kept_grads, blocks_turned, offsets, scale, 4)

        def x_or_y(z, x, c, y):
            return (z, 1 - x, c, y) if c == 0 else (z, x, c, 1 - y)

        def y_or_x(z, x, c, y):
            return (z, x, c, 1 - y) if c == 0 else (z, 1 - x, c, y)

        def z_far(z, x, c, y):
            return (z ^ 2, x, c, y)

        def z_near(z, x, c, y):
            return (z ^ 1, x, c, y)

        slot_id = lax.broadcasted_iota(jnp.int32, (1, offsets + 1, 1, 1), 1)

        def encode(part):
            bound = jnp.maximum(part[:, offsets:], 1e-30)
            exponent = jnp.ceil(jnp.log2(bound)) - 15.0
            values = part * jnp.exp2(-exponent)
            return jnp.where(slot_id < offsets, values, exponent).astype(jnp.float16)

        def decode(message):
            wide = message.astype(F32)
            unit = jnp.exp2(wide[:, offsets:])
            return jnp.where(slot_id < offsets, wide * unit, unit * 32768.0)

        near = near + exchange(far, cores)
        message, pair = encode(near[2:]), near[:2]
        message, pair, late_grads = lax.optimization_barrier((message, pair, kept_grads))
        spans = [(r * num_sent, num_sent) for r in range(5)]
        own_terms, inner_terms, first_terms, second_terms = input_terms(
            picks, late_grads, weights, [[spans[0], spans[3], spans[4]], [spans[1]], [spans[2]]]
        )
        back = exchange(inner_terms, cores)
        pair = pair + decode(exchange(message, x_or_y))
        message, part, own_terms = lax.optimization_barrier(
            (encode(pair[1:]), pair[:1], own_terms)
        )
        message = encode(part + decode(exchange(message, y_or_x)))
        message, back, late_picks = lax.optimization_barrier((message, back, picks))
        first_back = exchange(first_terms + back[num_sent : 2 * num_sent], straight)
        second_back = exchange(second_terms + back[2 * num_sent :], across)
        middle_block = num_blocks // 2
        upper = output_blocks(late_picks, weights, extended, (0, middle_block))
        part = decode(message) + decode(exchange(message, z_far))
        message, upper = lax.optimization_barrier((encode(part), upper))
        part = decode(message) + decode(exchange(message, z_near))
        message, first_back, second_back, late_picks = lax.optimization_barrier(
            (encode(part), first_back, second_back, late_picks)
        )
        output = output_blocks(
            late_picks, weights, extended, (middle_block, num_blocks), (upper,)
        )
        passed_back = exchange(second_back, cores)
        returned = [
            back[:num_sent] + jnp.where(middle, second_back + passed_back, 0.0),
            first_back,
        ]
        pair = jnp.concatenate([message, exchange(message, y_or_x)])
        pair, output, own_terms = lax.optimization_barrier((pair, output, own_terms))
        input_grad = input_grad_blocks(sent_ids, count, own_terms, returned)
        rest = exchange(pair, x_or_y)
        rest, input_grad = lax.optimization_barrier((rest, input_grad))
        messages = [pair, rest, exchange(pair, cores), exchange(rest, cores)]
        weight_grad = assemble(order, [decode(m) for m in messages])

    else:
        beside = [lax.ppermute(sent, "sy", route) for route in along_y]
        column = jnp.concatenate([sent] + beside, axis=0)
        from_inner = lax.ppermute(column, "sx", inner)
        from_outer = lax.ppermute(column, "sx", outer)
        extended = [blocks] + [to_blocks(a) for a in beside + [from_inner, from_outer]]
        order = jnp.concatenate([jnp.arange(8, dtype=jnp.int32)] * 2)
        parts = weight_terms(
            order, picks, kept_grads, [turned_own] + extended[1:], offsets, scale, 8
        )
        parts = jnp.swapaxes(parts[:, :offsets], 0, 1)
        weight_grad = lax.psum(parts.reshape(weights.shape), AXES)

        spans = [(r * num_sent, num_sent) for r in range(sides)]
        spans += [(sides * num_sent + r * per_x, per_x) for r in range(2)]
        own_terms, *halo_terms = input_terms(picks, grads, weights, [[span] for span in spans])
        inner_back = lax.ppermute(halo_terms[-2], "sx", inner)
        outer_back = lax.ppermute(halo_terms[-1], "sx", outer)
        returned = [inner_back[:num_sent], outer_back[:num_sent]]
        for number, route in enumerate(along_y):
            part = slice((1 + number) * num_sent, (2 + number) * num_sent)
            portion = halo_terms[number] + inner_back[part] + outer_back[part]
            returned.append(lax.ppermute(portion, "sy", [(j, i) for i, j in route]))
        output = output_blocks(picks, weights, extended, (0, num_blocks))
        input_grad = input_grad_blocks(sent_ids, count, own_terms, returned)

    return (output.reshape(features.shape), input_grad.reshape(features.shape), weight_grad)


def solution(mesh):
    tiles = P("dp", "sx", "sy", None, None)
    return jax.shard_map(
        local,
        mesh=mesh,
        in_specs=(tiles, tiles, P(), tiles, P("dp", "sx", "sy", None), P("dp", "sx", "sy")),
        out_specs=(tiles, tiles, P()),
        check_vma=False,
    )
```

```python
import functools
import math

import jax
import jax.numpy as jnp
from jax import lax
from jax.experimental import pallas as pl
from jax.experimental.pallas import tpu as pltpu
from jax.sharding import PartitionSpec as P

AXES = ("dp", "sx", "sy")
F32 = jnp.float32
BF16 = jnp.bfloat16
VMEM = pl.BlockSpec(memory_space=pltpu.VMEM)
SMEM = pl.BlockSpec(memory_space=pltpu.SMEM)
ANY = pl.BlockSpec(memory_space=pl.ANY)
HBM = pl.BlockSpec(memory_space=pltpu.HBM)


def params():
    return pltpu.CompilerParams(vmem_limit_bytes=12 * 2**20)


def cost(flops):
    return pl.CostEstimate(flops=flops, bytes_accessed=4 * 2**20, transcendentals=0)


def outgoing_kernel(sent_hbm, count_ref, x_ref, out_ref, sent_ref, sems):
    num_sent = out_ref.shape[0]
    copy = pltpu.make_async_copy(sent_hbm, sent_ref, sems.at[num_sent])
    copy.start()
    copy.wait()
    copies = [
        pltpu.make_async_copy(x_ref.at[sent_ref[s]], out_ref.at[s], sems.at[s])
        for s in range(num_sent)
    ]
    for copy in copies:
        copy.start()
    for copy in copies:
        copy.wait()
    for s in range(num_sent):

        @pl.when(sent_ref[s] >= count_ref[0])
        def _():
            out_ref[s] = jnp.zeros(out_ref.shape[1:], out_ref.dtype)


def outgoing(sent_ids, count, blocks):
    num_sent = sent_ids.shape[0]
    sent_ids, blocks = (
        pltpu.with_memory_space_constraint(a, pltpu.HBM) for a in (sent_ids, blocks)
    )
    return pl.pallas_call(
        outgoing_kernel,
        out_shape=jax.ShapeDtypeStruct((num_sent,) + blocks.shape[1:], blocks.dtype),
        in_specs=[HBM, SMEM, HBM],
        out_specs=VMEM,
        scratch_shapes=[
            pltpu.SMEM(sent_ids.shape, jnp.int32),
            pltpu.SemaphoreType.DMA((num_sent + 1,)),
        ],
        compiler_params=params(),
        cost_estimate=pl.CostEstimate(flops=0, bytes_accessed=2**18, transcendentals=0),
    )(sent_ids, count, blocks)


def input_terms_kernel(halo_spans, picks, grad_ref, weight_ref, own_ref, *rest):
    *halo_refs, accum = rest
    num_blocks, rows, channels = grad_ref.shape
    offsets = weight_ref.shape[0] // channels
    accum[...] = jnp.zeros_like(accum)

    def term(o, matrix):
        return lax.dot_general(
            grad_ref[o], matrix, (((1,), (1,)), ((), ())), preferred_element_type=F32
        )

    def two_offsets(pair, carry):
        start = pl.multiple_of(pair * 2 * channels, 2 * channels)
        matrix = weight_ref[pl.ds(start, 2 * channels), :]
        for o in range(num_blocks):
            both = term(o, matrix)
            accum[picks[o, 2 * pair]] += both[:, :channels]
            accum[picks[o, 2 * pair + 1]] += both[:, channels:]
        return carry

    lax.fori_loop(0, offsets // 2, two_offsets, 0)
    if offsets % 2:
        matrix = weight_ref[(offsets - 1) * channels :, :]
        for o in range(num_blocks):
            accum[picks[o, offsets - 1]] += term(o, matrix)
    own_ref[...] = accum[:num_blocks]
    for ref, spans in zip(halo_refs, halo_spans):
        to = 0
        for start, size in spans:
            ref[to : to + size] = accum[num_blocks + start : num_blocks + start + size]
            to += size


def input_terms(picks, grad, weights, halo_spans):
    num_blocks, rows, channels = grad.shape
    sizes = [num_blocks] + [sum(size for _, size in spans) for spans in halo_spans]
    return pl.pallas_call(
        functools.partial(input_terms_kernel, halo_spans),
        out_shape=[jax.ShapeDtypeStruct((n, rows, channels), F32) for n in sizes],
        in_specs=[SMEM, VMEM, VMEM],
        out_specs=[VMEM] * len(sizes),
        scratch_shapes=[pltpu.VMEM((sum(sizes) + 1, rows, channels), F32)],
        compiler_params=params(),
        cost_estimate=cost(10**7),
    )(picks, grad, weights.reshape(-1, channels))


def turn_kernel(block_ref, grad_ref, turned_ref, copy_ref):
    for e in range(block_ref.shape[0]):
        turned_ref[e] = block_ref[e].T
    copy_ref[...] = grad_ref[...]


def turn(blocks, grad):
    num_blocks, rows, channels = blocks.shape
    return pl.pallas_call(
        turn_kernel,
        out_shape=[
            jax.ShapeDtypeStruct((num_blocks, channels, rows), BF16),
            jax.ShapeDtypeStruct(grad.shape, BF16),
        ],
        in_specs=[VMEM, VMEM],
        out_specs=[VMEM, VMEM],
        compiler_params=params(),
        cost_estimate=cost(10**7),
    )(blocks, grad)


def weight_terms_kernel(scale, group, order_ref, picks, grad_ref, *rest):
    own_ref, *block_refs, out_ref, turned = rest
    channels = grad_ref.shape[1]
    rows = own_ref.shape[2]
    num_blocks = grad_ref.shape[0] // rows
    chunks, slots, size = out_ref.shape[:3]
    offsets = slots - 1
    start = own_ref.shape[0]
    turned[:start] = own_ref[...]
    for ref in block_refs:
        for e in range(ref.shape[0]):
            turned[start + e] = ref[e].T
        start += ref.shape[0]
    turned[start] = jnp.zeros(turned.shape[1:], turned.dtype)
    half = chunks * size
    lowest = order_ref[0]
    for r in range(1, chunks):
        lowest = jnp.minimum(lowest, order_ref[r])
    part = pl.ds(pl.multiple_of(lowest * size, half), half)

    def some_offsets(index, peak):
        wide = []
        for j in range(group):
            gathered = [turned[picks[o, index * group + j], part] for o in range(num_blocks)]
            wide.append(jnp.concatenate(gathered, axis=1))
        terms = jnp.dot(
            jnp.concatenate(wide, axis=0), grad_ref[...], preferred_element_type=F32
        )
        terms = (terms * scale).reshape(group, chunks, size, channels)
        for r in range(chunks):
            out_ref[order_ref[chunks + r], pl.ds(index * group, group)] = terms[:, r]
        return jnp.maximum(peak, jnp.max(jnp.abs(terms).reshape(-1, 8, channels), axis=0))

    peak = lax.fori_loop(
        0, offsets // group, some_offsets, jnp.zeros((8, channels), F32)
    )
    out_ref[:, offsets] = jnp.broadcast_to(jnp.max(peak), (chunks, size, channels))


def weight_terms(order, picks, grad, blocks, offsets, scale, chunks):
    num_blocks, rows, channels = grad.shape
    total = sum(b.shape[0] for b in blocks) + 1
    group = next(g for g in (9, 3, 1) if offsets % g == 0)
    size = channels // 8
    return pl.pallas_call(
        functools.partial(weight_terms_kernel, scale, group),
        out_shape=jax.ShapeDtypeStruct((chunks, offsets + 1, size, channels), F32),
        in_specs=[SMEM, SMEM, VMEM] + [VMEM] * len(blocks),
        out_specs=VMEM,
        scratch_shapes=[pltpu.VMEM((total, channels, rows), BF16)],
        compiler_params=params(),
        cost_estimate=cost(10**7),
    )(order, picks, grad.reshape(-1, channels), *blocks)


def output_kernel(group, span, done, picks, weight_ref, *rest):
    *block_refs, out_ref, held = rest
    if done:
        done_ref, *block_refs = block_refs
        out_ref[: done_ref.shape[0], :] = done_ref[...]
    total, rows, channels = held.shape
    offsets = weight_ref.shape[0] // channels
    start = 0
    for ref in block_refs:
        held[start : start + ref.shape[0]] = ref[...]
        start += ref.shape[0]
    held[start] = jnp.zeros(held.shape[1:], held.dtype)

    def some_blocks(index, carry):
        accum = jnp.zeros((group * rows, channels), F32)
        for k in range(0, offsets, 2):
            pair = range(k, min(k + 2, offsets))
            gathered = [
                jnp.concatenate(
                    [held[picks[index * group + j, kk]] for kk in pair], axis=1
                )
                for j in range(group)
            ]
            accum += jnp.dot(
                jnp.concatenate(gathered, axis=0),
                weight_ref[k * channels : (k + len(pair)) * channels, :],
                preferred_element_type=F32,
            )
        first = pl.multiple_of(index * group * rows, group * rows)
        out_ref[pl.ds(first, group * rows), :] = accum.astype(BF16)
        return carry

    lax.fori_loop(span[0] // group, span[1] // group, some_blocks, 0)


def output_blocks(picks, weights, blocks, span, done=()):
    _, rows, channels = blocks[0].shape
    total = sum(b.shape[0] for b in blocks) + 1
    group = next(g for g in (8, 6, 4, 2, 1) if span[0] % g == span[1] % g == 0)
    return pl.pallas_call(
        functools.partial(output_kernel, group, span, len(done)),
        out_shape=jax.ShapeDtypeStruct((span[1] * rows, channels), BF16),
        in_specs=[SMEM, VMEM] + [VMEM] * (len(done) + len(blocks)),
        out_specs=VMEM,
        scratch_shapes=[pltpu.VMEM((total, rows, channels), BF16)],
        compiler_params=params(),
        cost_estimate=cost(10**7),
    )(picks, weights.reshape(-1, channels), *done, *blocks)


def input_grad_kernel(sent_ref, count_ref, own_ref, *rest):
    *returned_refs, out_ref = rest
    num_blocks = own_ref.shape[0]
    for b in range(num_blocks):
        keep = jnp.where(b < count_ref[0], 1.0, 0.0)
        out_ref[b] = (own_ref[b] * keep).astype(BF16)
    for s in range(returned_refs[0].shape[0]):
        b = sent_ref[s]
        keep = jnp.where(b < count_ref[0], 1.0, 0.0)
        returned = returned_refs[0][s]
        for ref in returned_refs[1:]:
            returned = returned + ref[s]
        out_ref[b] = ((own_ref[b] + returned) * keep).astype(BF16)


def input_grad_blocks(sent_ids, count, own, returned):
    return pl.pallas_call(
        input_grad_kernel,
        out_shape=jax.ShapeDtypeStruct(own.shape, BF16),
        in_specs=[SMEM, SMEM, VMEM] + [VMEM] * len(returned),
        out_specs=VMEM,
        compiler_params=params(),
        cost_estimate=cost(10**7),
    )(sent_ids, count, own, *returned)


def assemble_kernel(order_ref, *rest):
    *piece_refs, out_ref, sems = rest
    if piece_refs[-1].shape == out_ref.shape:
        piece_refs = piece_refs[:-1]
    chunks = [ref.at[r] for ref in piece_refs for r in range(ref.shape[0])]
    size = chunks[0].shape[1]
    copies = []
    for r, chunk in enumerate(chunks):
        first = pl.multiple_of(order_ref[r] * size, size)
        copies.append(
            pltpu.make_async_copy(
                chunk.at[: out_ref.shape[0]], out_ref.at[:, pl.ds(first, size)], sems.at[r]
            )
        )
    for copy in copies:
        copy.start()
    for copy in copies:
        copy.wait()


def assemble(order, pieces, shape, into=()):
    count = sum(p.shape[0] for p in pieces)
    return pl.pallas_call(
        assemble_kernel,
        out_shape=jax.ShapeDtypeStruct(shape, F32),
        in_specs=[SMEM] + [ANY] * (len(pieces) + len(into)),
        out_specs=ANY,
        scratch_shapes=[pltpu.SemaphoreType.DMA((count,))],
        input_output_aliases={1 + len(pieces): 0} if into else {},
        compiler_params=params(),
    )(order, *pieces, *into)


def local(features, cotangent, weights, tables, send_lists, counts):
    num_blocks = tables.shape[4]
    num_sent = send_lists.shape[3]
    offsets, channels = weights.shape[0], weights.shape[1]
    width = features.shape[3] // num_blocks
    size_z, size_x, size_y = (lax.axis_size(a) for a in AXES)
    scene, tile_x, tile_y = (lax.axis_index(a) for a in AXES)
    blocks = features.reshape(num_blocks, width, channels)
    grads = cotangent.reshape(num_blocks, width, channels)
    sent_ids = send_lists.reshape(num_sent)
    count = counts.reshape(1)

    odd = tile_x % 2
    inner = [(i, i ^ 1) for i in range(size_x) if (i ^ 1) < size_x]
    outer = [(i, i + 1) for i in range(1, size_x - 1, 2)]
    outer = outer + [(j, i) for i, j in outer]
    if size_y == 2:
        along_y = [[(0, 1), (1, 0)]]
    else:
        along_y = [
            [(i, i + 1) for i in range(size_y - 1)],
            [(i + 1, i) for i in range(size_y - 1)],
        ]
    sides = len(along_y)
    per_x = (1 + sides) * num_sent
    paired = (size_z, size_x, size_y) == (4, 4, 2)

    def to_blocks(array):
        return array.reshape(-1, width, channels)

    def to_rows(array):
        return array.reshape(-1, channels)

    table = tables.reshape(offsets, num_blocks).T
    code = table - num_blocks
    number = code // num_sent
    cell = number + (number >= 4)
    step_x, step_y = cell // 3 - 1, cell % 3 - 1
    slot = code % num_sent
    near_x, near_y = tile_x + step_x, tile_y + step_y
    inside = (near_x >= 0) & (near_x < size_x) & (near_y >= 0) & (near_y < size_y)
    if size_y == 2:
        side = (step_y != 0).astype(jnp.int32)
    else:
        side = jnp.where(step_y == 0, 0, jnp.where(step_y < 0, 1, 2))
    toward = 1 - 2 * odd
    if paired:
        middle = (tile_x == 1) | (tile_x == 2)
        to_inner = jnp.where(side == 0, 0, jnp.where(middle, 3, 2))
        place = jnp.where(
            step_x == 0, jnp.where(middle, 4, 1), jnp.where(step_x == toward, to_inner, 1 + side)
        )
        place = num_blocks + place * num_sent + slot
        empty = num_blocks + 5 * num_sent
    else:
        beyond_x = jnp.where(step_x == toward, 0, per_x) + (sides + side) * num_sent + slot
        place = num_blocks + jnp.where(step_x == 0, (side - 1) * num_sent + slot, beyond_x)
        empty = num_blocks + sides * num_sent + 2 * per_x
    is_own = table < num_blocks
    is_empty = table >= num_blocks + 8 * num_sent
    place = jnp.where(is_own, table, place)
    dead = jnp.where(is_own, table >= count[0], is_empty | ~inside)
    dead = dead | (jnp.arange(num_blocks)[:, None] >= count[0])
    picks = jnp.where(dead, empty, place).astype(jnp.int32)

    sent = to_rows(outgoing(sent_ids, count, blocks))
    turned_own, kept_grads = turn(blocks, grads)
    scale = 1.0 / math.sqrt(num_blocks * width * size_z * size_x * size_y)
    if paired:

        def flat(z, x, c, y):
            return (z * size_x + 2 * x + c) * size_y + y

        def exchange(array, to):
            places = [
                (z, x, c, y) for z in range(4) for x in range(2) for c in range(2) for y in range(2)
            ]
            route = [(flat(*p), flat(*to(*p))) for p in places]
            return lax.ppermute(array, AXES, route)

        def cores(z, x, c, y):
            return z, x, 1 - c, y

        def is_middle(z, x, c, y):
            return x != c

        def straight(z, x, c, y):
            return (z, 1 - x, 1 - c, y) if is_middle(z, x, c, y) else (z, x, c, 1 - y)

        def across(z, x, c, y):
            return (z, 1 - x, 1 - c, 1 - y) if is_middle(z, x, c, y) else (z, x, c, 1 - y)

        beside = exchange(sent, cores)
        first = exchange(sent, straight)
        second = exchange(jnp.where(middle, sent, beside), across)
        second, turned_own = lax.optimization_barrier((second, turned_own))
        passed = [exchange(first, cores), exchange(second, cores)]
        extended = [blocks] + [to_blocks(a) for a in [beside, first, second] + passed]

        core, far_x = odd, tile_x // 2
        chunk = jnp.arange(4, dtype=jnp.int32)
        low = far_x * 2 + tile_y
        swapped = (chunk % 2) * 2 + chunk // 2
        mine = jnp.where(core == 0, chunk, swapped)
        theirs = jnp.where(core == 0, swapped, chunk)
        keep, send = core * 4 + (low ^ mine), (1 - core) * 4 + (low ^ theirs)

        def places(bits):
            moved = chunk ^ low
            return jnp.where(bits == 0, moved, (moved % 2) * 2 + moved // 2)

        near_order = jnp.concatenate([core * 4 + chunk, places(core)])
        far_order = jnp.concatenate([(1 - core) * 4 + chunk, places(1 - core)])
        blocks_turned = [turned_own] + extended[1:]
        far = weight_terms(far_order, picks, kept_grads, blocks_turned, offsets, scale, 4)
        kept_grads, far = lax.optimization_barrier((kept_grads, far))
        near = weight_terms(near_order, picks, kept_grads, blocks_turned, offsets, scale, 4)

        def x_or_y(z, x, c, y):
            return (z, 1 - x, c, y) if c == 0 else (z, x, c, 1 - y)

        def y_or_x(z, x, c, y):
            return (z, x, c, 1 - y) if c == 0 else (z, 1 - x, c, y)

        def z_far(z, x, c, y):
            return (z ^ 2, x, c, y)

        def z_near(z, x, c, y):
            return (z ^ 1, x, c, y)

        slot_id = lax.broadcasted_iota(jnp.int32, (1, offsets + 1, 1, 1), 1)

        def encode(part):
            bound = jnp.maximum(part[:, offsets:], 1e-30)
            exponent = jnp.ceil(jnp.log2(bound)) - 15.0
            values = part * jnp.exp2(-exponent)
            return jnp.where(slot_id < offsets, values, exponent).astype(jnp.float16)

        def decode(message):
            wide = message.astype(F32)
            unit = jnp.exp2(wide[:, offsets:])
            return jnp.where(slot_id < offsets, wide * unit, unit * 32768.0)

        near = near + decode(exchange(encode(far), cores))
        message, pair = encode(near[2:]), near[:2]
        message, pair, late_grads = lax.optimization_barrier((message, pair, kept_grads))
        spans = [(r * num_sent, num_sent) for r in range(5)]
        own_terms, inner_terms, first_terms, second_terms = input_terms(
            picks, late_grads, weights, [[spans[0], spans[3], spans[4]], [spans[1]], [spans[2]]]
        )
        back = exchange(inner_terms, cores)
        pair = pair + decode(exchange(message, x_or_y))
        message, part, own_terms, late_picks = lax.optimization_barrier(
            (encode(pair[1:]), pair[:1], own_terms, picks)
        )
        cuts = [num_blocks * third // 24 * 8 for third in range(3)] + [num_blocks]
        output = output_blocks(late_picks, weights, extended, (cuts[0], cuts[1]))
        message = encode(part + decode(exchange(message, y_or_x)))
        message, back, late_picks, output = lax.optimization_barrier(
            (message, back, late_picks, output)
        )
        first_back = exchange(first_terms + back[num_sent : 2 * num_sent], straight)
        second_back = exchange(second_terms + back[2 * num_sent :], across)
        output = output_blocks(late_picks, weights, extended, (cuts[1], cuts[2]), (output,))
        part = decode(message) + decode(exchange(message, z_far))
        message, output = lax.optimization_barrier((encode(part), output))
        part = decode(message) + decode(exchange(message, z_near))
        message, first_back, second_back, late_picks = lax.optimization_barrier(
            (encode(part), first_back, second_back, late_picks)
        )
        output = output_blocks(late_picks, weights, extended, (cuts[2], cuts[3]), (output,))
        passed_back = exchange(second_back, cores)
        returned = [
            back[:num_sent] + jnp.where(middle, second_back + passed_back, 0.0),
            first_back,
        ]
        pair = jnp.concatenate([message, exchange(message, y_or_x)])
        pair, output, own_terms = lax.optimization_barrier((pair, output, own_terms))
        input_grad = input_grad_blocks(sent_ids, count, own_terms, returned)
        early_order = jnp.concatenate([keep[:2], send[:2]])
        late_order = jnp.concatenate([keep[2:], send[2:]])
        early = [decode(m) for m in (pair, exchange(pair, cores))]
        weight_grad = assemble(early_order, early, weights.shape)
        rest = exchange(pair, x_or_y)
        rest, input_grad, weight_grad = lax.optimization_barrier((rest, input_grad, weight_grad))
        late = [decode(m) for m in (rest, exchange(rest, cores))]
        weight_grad = assemble(late_order, late, weights.shape, [weight_grad])

    else:
        beside = [lax.ppermute(sent, "sy", route) for route in along_y]
        column = jnp.concatenate([sent] + beside, axis=0)
        from_inner = lax.ppermute(column, "sx", inner)
        from_outer = lax.ppermute(column, "sx", outer)
        extended = [blocks] + [to_blocks(a) for a in beside + [from_inner, from_outer]]
        order = jnp.concatenate([jnp.arange(8, dtype=jnp.int32)] * 2)
        parts = weight_terms(
            order, picks, kept_grads, [turned_own] + extended[1:], offsets, scale, 8
        )
        parts = jnp.swapaxes(parts[:, :offsets], 0, 1)
        weight_grad = lax.psum(parts.reshape(weights.shape), AXES)

        spans = [(r * num_sent, num_sent) for r in range(sides)]
        spans += [(sides * num_sent + r * per_x, per_x) for r in range(2)]
        own_terms, *halo_terms = input_terms(picks, grads, weights, [[span] for span in spans])
        inner_back = lax.ppermute(halo_terms[-2], "sx", inner)
        outer_back = lax.ppermute(halo_terms[-1], "sx", outer)
        returned = [inner_back[:num_sent], outer_back[:num_sent]]
        for number, route in enumerate(along_y):
            part = slice((1 + number) * num_sent, (2 + number) * num_sent)
            portion = halo_terms[number] + inner_back[part] + outer_back[part]
            returned.append(lax.ppermute(portion, "sy", [(j, i) for i, j in route]))
        output = output_blocks(picks, weights, extended, (0, num_blocks))
        input_grad = input_grad_blocks(sent_ids, count, own_terms, returned)

    return (output.reshape(features.shape), input_grad.reshape(features.shape), weight_grad)


def solution(mesh):
    tiles = P("dp", "sx", "sy", None, None)
    return jax.shard_map(
        local,
        mesh=mesh,
        in_specs=(tiles, tiles, P(), tiles, P("dp", "sx", "sy", None), P("dp", "sx", "sy")),
        out_specs=(tiles, tiles, P()),
        check_vma=False,
    )
```
